32 devices in a mesh: depth: 4 (over z), tile: 8 (over y, x, core).
Axes of the slice: x: 2, y: 2, z: 4, core: 2. Of those that a mesh axis runs over, the one named last changes fastest.
Arguments:
- volume_field: bfloat16 [128, 256, 1024], P('depth', 'tile'), may hold values from -6 to 6
- ray_near: int32 [256, 1024], P('tile'), may hold values from 0 to 31
- ray_far: int32 [256, 1024], P('tile'), may hold values from 96 to 128
- tf_color: float32 [3, 16], replicated, may hold values from 0 to 1
- tf_opacity: float32 [16], replicated, may hold values from 0.2 to 40
- knot_count: int32 [1], replicated, may hold values from 4 to 16
Outputs:
- image_rgba: float32 [4, 256, 1024], P(None, 'tile', 'depth')
The draws below stay inside these ranges and needn't reach their ends.
All inputs are finite; a program needn't handle non-finite values.
Results may differ from the reference program's by a relative error of at most 0.0003.
Values may be sent and summed in bfloat16 or wider, within the bound.
A program may use at most 64 MiB of HBM per device.

```python
import math
import jax
import jax.numpy as jnp
from jax import lax

TH = 32
IW = 1024
KNOTS = 16
NZ = 128
IH = 256


def wave_sum(key):
    keys = jax.random.split(key, 2)
    period = jax.random.uniform(keys[0], (3,), jnp.float32, 16.0, 32.0)
    phase = jax.random.uniform(keys[1], (3,), jnp.float32, 0.0, 2.0 * math.pi)
    depth_pos = jnp.arange(NZ, dtype=jnp.float32)[:, None, None]
    row_pos = jnp.arange(IH, dtype=jnp.float32)[None, :, None]
    column_pos = jnp.arange(IW, dtype=jnp.float32)[None, None, :]
    wave_depth = jnp.cos(2.0 * math.pi * depth_pos / period[0] + phase[0])
    wave_row = jnp.cos(2.0 * math.pi * row_pos / period[1] + phase[1])
    wave_column = jnp.cos(2.0 * math.pi * column_pos / period[2] + phase[2])
    return wave_depth + wave_row + wave_column


def draw_volume_field(key, part):
    key = jax.random.fold_in(key, 11)
    keys = jax.random.split(key, 2)
    waves = wave_sum(keys[0])
    rough = 0.8 * jax.random.normal(keys[1], (NZ, IH, IW), jnp.float32)
    field = 0.8 * waves + rough
    return jnp.clip(field, -6.0, 6.0).astype(jnp.bfloat16)


def draw_tf_opacity(key, part):
    key = jax.random.fold_in(key, 23)
    keys = jax.random.split(key, 2)
    others = jnp.exp(jax.random.uniform(keys[0], (KNOTS,), jnp.float32, math.log(0.2), math.log(6.0)))
    front = jax.random.uniform(keys[1], (), jnp.float32, 24.0, 40.0)
    first_knot = jnp.arange(KNOTS, dtype=jnp.int32) == 0
    return jnp.where(first_knot, front, others).astype(jnp.float32)


def with_ends(entries, key, least, largest):
    dims = entries.shape
    spot = [jax.random.randint(jax.random.fold_in(key, axis), (), 0, dims[axis]) for axis in range(len(dims))]
    entries = entries.at[tuple(spot)].set(least)
    longest = dims.index(max(dims))
    spot[longest] = (spot[longest] + 1) % dims[longest]
    return entries.at[tuple(spot)].set(largest)


def setup_inputs(seed: int = 0) -> dict:
    splits = jax.random.split(jax.random.key(seed), 7)
    volume_field = draw_volume_field(jax.random.fold_in(splits[6], 71), 0)
    ray_near = with_ends(jax.random.randint(splits[1], (IH, IW), 0, NZ // 4), jax.random.fold_in(splits[1], 1), 0, (NZ // 4) - 1).astype(jnp.int32)
    ray_far = with_ends(jax.random.randint(splits[2], (IH, IW), NZ - NZ // 4, NZ + 1), jax.random.fold_in(splits[2], 1), NZ - NZ // 4, NZ).astype(jnp.int32)
    tf_color = jnp.clip(jax.random.uniform(splits[3], (3, KNOTS), jnp.float32, 0.0, 1.0), 0.0, 1.0)
    tf_opacity = draw_tf_opacity(jax.random.fold_in(splits[6], 71), 0)
    knot_count = jax.random.randint(splits[5], (1,), 4, KNOTS + 1).astype(jnp.int32)
    return dict(volume_field=volume_field, ray_near=ray_near, ray_far=ray_far, tf_color=tf_color, tf_opacity=tf_opacity, knot_count=knot_count)


def smooth(padded):
    padded = 0.25 * padded[:-2] + 0.5 * padded[1:-1] + 0.25 * padded[2:]
    padded = 0.25 * padded[:, :-2] + 0.5 * padded[:, 1:-1] + 0.25 * padded[:, 2:]
    padded = 0.25 * padded[:, :, :-2] + 0.5 * padded[:, :, 1:-1] + 0.25 * padded[:, :, 2:]
    return padded

def shade_lookup(extended, depth_index, ray_near, ray_far, tf_color, tf_opacity, knot_span, step_len):
    smoothed = smooth(extended)
    center = smoothed[1:-1, 1:-1, 1:-1]
    grad_z = 0.5 * (smoothed[2:, 1:-1, 1:-1] - smoothed[:-2, 1:-1, 1:-1])
    grad_y = 0.5 * (smoothed[1:-1, 2:, 1:-1] - smoothed[1:-1, :-2, 1:-1])
    grad_x = 0.5 * (smoothed[1:-1, 1:-1, 2:] - smoothed[1:-1, 1:-1, :-2])
    facing = 8.0 * (0.48 * grad_z + 0.6 * grad_y + 0.64 * grad_x)
    magnitude = 64.0 * (grad_z * grad_z + grad_y * grad_y + grad_x * grad_x)
    shading = 0.25 + 0.75 * jnp.abs(facing) / jnp.sqrt(magnitude + 1.0)
    tf_level = (0.5 + 0.5 * jnp.tanh(3.0 * center)) * knot_span
    color_red = jnp.zeros_like(center)
    color_green = jnp.zeros_like(center)
    color_blue = jnp.zeros_like(center)
    extinction = jnp.zeros_like(center)
    for knot in range(KNOTS):
        tf_weight = jnp.maximum(0.0, 1.0 - jnp.abs(tf_level - float(knot)))
        color_red = color_red + tf_color[0, knot] * tf_weight
        color_green = color_green + tf_color[1, knot] * tf_weight
        color_blue = color_blue + tf_color[2, knot] * tf_weight
        extinction = extinction + tf_opacity[knot] * tf_weight
    inside = (depth_index[:, None, None] >= ray_near[None]) & (depth_index[:, None, None] < ray_far[None])
    depth_od = jnp.where(inside, extinction * step_len, jnp.float32(0.0))
    absorbed = (1.0 - jnp.exp(-depth_od)) * shading
    emitted = jnp.stack([color_red * absorbed, color_green * absorbed, color_blue * absorbed])
    return (depth_od, emitted)

def reference(volume_field, ray_near, ray_far, tf_color, tf_opacity, knot_count):
    padded = jnp.pad(volume_field, 2)
    knot_span = knot_count[0].astype(jnp.float32) - 1.0
    step_len = jnp.float32(1.0 / NZ)
    depth_index = jnp.arange(NZ, dtype=jnp.int32)

    def render_rows(row_block):
        first = (row_block * TH).astype(jnp.int32)
        zero = jnp.zeros((), jnp.int32)
        extended = lax.dynamic_slice(padded, (zero, first, zero), (NZ + 4, TH + 4, IW + 4)).astype(jnp.float32)
        near_rows = lax.dynamic_slice(ray_near, (first, zero), (TH, IW))
        far_rows = lax.dynamic_slice(ray_far, (first, zero), (TH, IW))
        depth_od, emitted = shade_lookup(extended, depth_index, near_rows, far_rows, tf_color, tf_opacity, knot_span, step_len)
        depth_before = jnp.cumsum(depth_od, axis=0) - depth_od
        color_out = lax.optimization_barrier(jnp.sum(emitted * jnp.exp(-depth_before)[None], axis=1))
        opacity_out = 1.0 - jnp.exp(-lax.optimization_barrier(jnp.sum(depth_od, axis=0)))
        return jnp.concatenate([color_out, opacity_out[None]], axis=0)
    blocks = lax.map(render_rows, jnp.arange(IH // TH, dtype=jnp.int32))
    return jnp.transpose(blocks, (1, 0, 2, 3)).reshape(4, IH, IW)
```

```python
import functools
import math

import jax
import jax.numpy as jnp
from jax import lax
from jax.experimental import pallas as pl
from jax.experimental.pallas import tpu as pltpu
from jax.sharding import PartitionSpec as P

KNOTS = 16
LANES = 128
ROWS = 8
PAD = 8


def x_window(tile, tiles):
    return max(tile - 1, 0), min(tile + 2, tiles)


def x_filters(tile, tiles):
    first, last = x_window(tile, tiles)
    shape = ((last - first) * LANES, LANES)
    source = lax.broadcasted_iota(jnp.int32, shape, 0) + (first - tile) * LANES
    offset = source - lax.broadcasted_iota(jnp.int32, shape, 1)
    distance = jnp.abs(offset)
    smooth = jnp.where(distance == 0, 0.125, jnp.where(distance == 1, 0.0625, 0.0))
    slope = jnp.where(distance == 1, 0.125, jnp.where(distance == 2, 0.0625, 0.0))
    slope = jnp.where(offset < 0, -slope, slope)
    return jnp.concatenate([smooth, slope], axis=1).astype(jnp.bfloat16)


def render_kernel(
    planes, slabs, color_ref, opacity_ref, knots_ref, near_ref, far_ref, field_ref, out_ref,
    smooth_ref, slope_ref,
):
    tiles = field_ref.shape[2] // LANES
    padded_rows = field_ref.shape[1]
    per_slab = tiles // slabs
    total = field_ref.shape[0]
    group = 4

    for tile in range(tiles):
        first, last = x_window(tile, tiles)
        filters = x_filters(tile, tiles)

        @pl.loop(0, total // group)
        def _(step, tile=tile, first=first, last=last, filters=filters):
            start = step * group
            window = field_ref[pl.ds(start, group), :, first * LANES : last * LANES]
            window = window.reshape(group * padded_rows, (last - first) * LANES)
            both = jnp.dot(window, filters, preferred_element_type=jnp.float32)
            both = both.reshape(group, padded_rows, 2 * LANES)
            smooth_ref[tile, pl.ds(start, group)] = both[:, :, :LANES]
            slope_ref[tile, pl.ds(start, group)] = both[:, :, LANES:]

    half_span = (knots_ref[0].astype(jnp.float32) - 1.0) * 0.5
    lane = lax.broadcasted_iota(jnp.int32, (ROWS, LANES), 1)
    tables = []
    scale = -math.log2(math.e) / (planes * slabs)
    for channel in range(4):
        if channel < 3:
            knot = [color_ref[channel, k] for k in range(KNOTS)]
        else:
            knot = [opacity_ref[k] * scale for k in range(KNOTS)]
        base = jnp.full((ROWS, LANES), knot[KNOTS - 1], jnp.float32)
        slope = jnp.zeros((ROWS, LANES), jnp.float32)
        for k in range(KNOTS - 1):
            rise = knot[k + 1] - knot[k]
            base = jnp.where(lane == k, knot[k] - k * rise, base)
            slope = jnp.where(lane == k, rise, slope)
        tables.append((base, slope))

    first_plane = lax.axis_index("depth") * planes

    def pick(table, index):
        return jnp.take_along_axis(table, index, axis=1, mode="promise_in_bounds")

    row_blocks = near_ref.shape[0] // ROWS

    @pl.loop(0, tiles * row_blocks)
    def _(cell):
        tile = cell // row_blocks
        row = pl.multiple_of((cell % row_blocks) * ROWS, ROWS)
        column = pl.multiple_of(tile * LANES, LANES)
        near = near_ref[pl.ds(row, ROWS), pl.ds(column, LANES)] - first_plane
        far = far_ref[pl.ds(row, ROWS), pl.ds(column, LANES)] - first_plane

        def y_pass(plane):
            at = lambda ref, dy: ref[tile, plane, pl.ds(row + (PAD + dy), ROWS), :]
            mid, up, down = at(smooth_ref, 0), at(smooth_ref, 1), at(smooth_ref, -1)
            level = (up + down) + (mid + mid)
            step = up - down
            rise = (at(smooth_ref, 2) - at(smooth_ref, -2)) + (step + step)
            mid = at(slope_ref, 0)
            across = (at(slope_ref, 1) + at(slope_ref, -1)) + (mid + mid)
            return level, rise, across

        y = [y_pass(0)]
        pairs = []
        smooth = []
        seen = jnp.ones((ROWS, LANES), jnp.float32)
        image = [jnp.zeros((ROWS, LANES), jnp.float32) for _ in range(3)]
        for plane in range(1, total):
            y.append(y_pass(plane))
            pairs.append(tuple(a + b for a, b in zip(y[plane - 1], y[plane])))
            y[plane - 1] = None
            if plane < 2:
                continue
            smooth.append(pairs[plane - 2][0] + pairs[plane - 1][0])
            if plane < 4:
                continue
            z = plane - 4
            center = smooth[z + 1]
            grad_z = smooth[z + 2] - smooth[z]
            grad_y = pairs[z + 1][1] + pairs[z + 2][1]
            grad_x = pairs[z + 1][2] + pairs[z + 2][2]
            facing = 0.36 * grad_z + 0.45 * grad_y + 0.48 * grad_x
            magnitude = grad_z * grad_z + grad_y * grad_y + (grad_x * grad_x + 1.0)
            shading = 0.25 + jnp.abs(facing) * lax.rsqrt(magnitude)
            tf_level = jnp.tanh(0.75 * center) * half_span + half_span
            index = tf_level.astype(jnp.int32)
            color = [pick(base, index) + pick(slope, index) * tf_level for base, slope in tables]
            inside = (near <= z) & (far > z)
            through = jnp.exp2(jnp.where(inside, color[3], 0.0))
            after = seen * through
            weight = (seen - after) * shading
            seen = after
            image = [total_ + c * weight for total_, c in zip(image, color)]
        slab = tile // per_slab
        inner = pl.multiple_of((tile % per_slab) * LANES, LANES)
        for channel, value in enumerate(image + [seen]):
            out_ref[slab, channel, pl.ds(row, ROWS), pl.ds(inner, LANES)] = value


def neighbours(block, axis, dim, width):
    count = lax.axis_size(axis)
    forward = [(i, i + 1) for i in range(count - 1)]
    backward = [(i + 1, i) for i in range(count - 1)]
    size = block.shape[dim]
    low = lax.ppermute(lax.slice_in_dim(block, size - width, size, axis=dim), axis, forward)
    high = lax.ppermute(lax.slice_in_dim(block, 0, width, axis=dim), axis, backward)
    return low, high


def on_device(volume_field, ray_near, ray_far, tf_color, tf_opacity, knot_count):
    planes, rows, columns = volume_field.shape
    slabs = lax.axis_size("depth")
    low, high = neighbours(volume_field, "depth", 0, 2)
    field = jnp.concatenate([low, volume_field, high], axis=0)
    low, high = neighbours(field, "tile", 1, 2)
    rim = jnp.zeros((planes + 4, PAD - 2, columns), field.dtype)
    field = jnp.concatenate([rim, low, field, high, rim], axis=1)
    tiles = columns // LANES
    smem = pl.BlockSpec(memory_space=pltpu.SMEM)
    vmem = pl.BlockSpec(memory_space=pltpu.VMEM)
    local = pl.pallas_call(
        functools.partial(render_kernel, planes, slabs),
        out_shape=jax.ShapeDtypeStruct((slabs, 4, rows, columns // slabs), jnp.float32),
        in_specs=[smem, smem, smem, vmem, vmem, vmem],
        out_specs=vmem,
        scratch_shapes=[
            pltpu.VMEM((tiles, planes + 4, rows + 2 * PAD, LANES), jnp.float32),
            pltpu.VMEM((tiles, planes + 4, rows + 2 * PAD, LANES), jnp.float32),
        ],
        compiler_params=pltpu.CompilerParams(vmem_limit_bytes=40 * 1024 * 1024),
    )(tf_color, tf_opacity, knot_count, ray_near, ray_far, field)
    every = lax.all_to_all(local, "depth", 0, 0, tiled=True)
    color, seen = every[slabs - 1, :3], every[slabs - 1, 3]
    for slab in range(slabs - 2, -1, -1):
        color = every[slab, :3] + every[slab, 3] * color
        seen = every[slab, 3] * seen
    return jnp.concatenate([color, (1.0 - seen)[None]], axis=0)


def solution(mesh):
    return jax.shard_map(
        on_device,
        mesh=mesh,
        in_specs=(P("depth", "tile", None), P("tile", None), P("tile", None), P(), P(), P()),
        out_specs=P(None, "tile", "depth"),
        check_vma=False,
    )
```

```python
import functools
import math

import jax
import jax.numpy as jnp
from jax import lax
from jax.experimental import pallas as pl
from jax.experimental.pallas import tpu as pltpu
from jax.sharding import PartitionSpec as P

KNOTS = 16
LANES = 128
ROWS = 8
PAD = 8
MESH = pl.DeviceIdType.MESH


def x_window(tile, tiles):
    return max(tile - 1, 0), min(tile + 2, tiles)


def x_filters(tile, tiles):
    first, last = x_window(tile, tiles)
    shape = ((last - first) * LANES, LANES)
    source = lax.broadcasted_iota(jnp.int32, shape, 0) + (first - tile) * LANES
    offset = source - lax.broadcasted_iota(jnp.int32, shape, 1)
    distance = jnp.abs(offset)
    smooth = jnp.where(distance == 0, 0.125, jnp.where(distance == 1, 0.0625, 0.0))
    slope = jnp.where(distance == 1, 0.125, jnp.where(distance == 2, 0.0625, 0.0))
    slope = jnp.where(offset < 0, -slope, slope)
    return jnp.concatenate([smooth, slope], axis=1).astype(jnp.bfloat16)


def render_kernel(
    axes, color_ref, opacity_ref, knots_ref, near_hbm, far_hbm, edge_hbm, field_hbm, out_ref,
    field_ref, near_ref, far_ref, z_rim, y_rim, corner, smooth_ref, slope_ref, part_ref, all_ref,
    local_sem, rim_send, rim_recv, part_send, part_recv,
):
    slabs, strips = axes
    planes, rows, columns = field_ref.shape
    tiles = columns // LANES
    per_slab = tiles // slabs
    total = planes + 4
    padded_rows = rows + 2 * PAD
    slab, strip = lax.axis_index("depth"), lax.axis_index("tile")
    moves = [(dz, dy) for dz in (-1, 0, 1) for dy in (-1, 0, 1) if dz or dy]

    def exists(dz, dy):
        ok = None
        for step, mine, count in ((dz, slab, slabs), (dy, strip, strips)):
            if step:
                test = mine > 0 if step < 0 else mine < count - 1
                ok = test if ok is None else ok & test
        return ok

    locals_ = [
        pltpu.make_async_copy(source, target, local_sem.at[i])
        for i, (source, target) in enumerate(
            ((field_hbm, field_ref), (near_hbm, near_ref), (far_hbm, far_ref))
        )
    ]
    for copy in locals_:
        copy.start()

    barrier = pltpu.get_barrier_semaphore()
    arrivals = slabs - 1
    for step in range(1, slabs):
        pl.semaphore_signal(
            barrier, inc=1, device_id=(lax.rem(slab + step, slabs), strip), device_id_type=MESH
        )
    for dz, dy in moves:
        if dy:
            ok = exists(dz, dy)
            arrivals = arrivals + jnp.where(ok, 1, 0)

            @pl.when(ok)
            def _(dz=dz, dy=dy):
                pl.semaphore_signal(
                    barrier, inc=1, device_id=(slab + dz, strip + dy), device_id_type=MESH
                )
    pl.semaphore_wait(barrier, arrivals)

    def rim(dz, dy, number, target):
        z_side, y_side = (0 if dz > 0 else 1), (0 if dy > 0 else 1)
        if not dy:
            source = field_hbm.at[pl.ds(planes - 2 if dz > 0 else 0, 2)]
            place = z_rim.at[z_side]
        elif not dz:
            source, place = edge_hbm.at[1 - y_side], y_rim.at[y_side]
        else:
            source = edge_hbm.at[1 - y_side, :, pl.ds(planes - 16 if dz > 0 else 0, 16)]
            place = corner.at[z_side, y_side]
        return pltpu.make_async_remote_copy(
            src_ref=source, dst_ref=place, send_sem=rim_send.at[number],
            recv_sem=rim_recv.at[number], device_id=target, device_id_type=MESH,
        )

    for number, (dz, dy) in enumerate(moves):
        @pl.when(exists(dz, dy))
        def _(dz=dz, dy=dy, number=number):
            rim(dz, dy, number, (slab + dz, strip + dy)).start()

        @pl.when(jnp.logical_not(exists(-dz, -dy)))
        def _(dz=dz, dy=dy):
            z_side, y_side = (0 if dz > 0 else 1), (0 if dy > 0 else 1)
            if not dy:
                z_rim[z_side] = jnp.zeros(z_rim.shape[1:], z_rim.dtype)
            elif not dz:
                y_rim[y_side] = jnp.zeros(y_rim.shape[1:], y_rim.dtype)
            else:
                corner[z_side, y_side] = jnp.zeros(corner.shape[2:], corner.dtype)

    locals_[0].wait()
    group = 4
    for tile in range(tiles):
        first, last = x_window(tile, tiles)
        filters = x_filters(tile, tiles)

        @pl.loop(0, planes // group)
        def _(step, tile=tile, first=first, last=last, filters=filters):
            start = step * group
            window = field_ref[pl.ds(start, group), :, first * LANES : last * LANES]
            window = window.reshape(group * rows, (last - first) * LANES)
            both = jnp.dot(window, filters, preferred_element_type=jnp.float32)
            for i in range(group):
                at = pl.ds((start + (2 + i)) * padded_rows + PAD, rows)
                piece = both[i * rows : (i + 1) * rows]
                smooth_ref[tile, at, :] = piece[:, :LANES]
                slope_ref[tile, at, :] = piece[:, LANES:]

    for number, (dz, dy) in enumerate(moves):
        @pl.when(exists(-dz, -dy))
        def _(dz=dz, dy=dy, number=number):
            rim(dz, dy, number, (slab - dz, strip - dy)).wait_recv()

    for tile in range(tiles):
        first, last = x_window(tile, tiles)
        filters = x_filters(tile, tiles)
        lanes = slice(first * LANES, last * LANES)

        def filtered(window):
            window = window.reshape(-1, window.shape[-1])
            return jnp.dot(window, filters, preferred_element_type=jnp.float32)

        def put(at, piece, tile=tile):
            smooth_ref[tile, at, :] = piece[:, :LANES]
            slope_ref[tile, at, :] = piece[:, LANES:]

        both = filtered(z_rim[:, :, :, lanes])
        for i, plane in enumerate((0, 1, planes + 2, planes + 3)):
            put(pl.ds(plane * padded_rows + PAD, rows), both[i * rows : (i + 1) * rows])
        both = filtered(y_rim[:, :, :, lanes])
        spots = (PAD - 2, PAD - 1, PAD + rows, PAD + rows + 1)
        for i, spot in enumerate(spots):
            put(
                pl.ds(2 * padded_rows + spot, planes, stride=padded_rows),
                both[i * planes : (i + 1) * planes],
            )
        both = filtered(corner[:, :, :, :, lanes])
        for z_side in range(2):
            for i, spot in enumerate(spots):
                for p in range(2):
                    plane = p if z_side == 0 else planes + 2 + p
                    line = (z_side * 4 + i) * 16 + (14 + p if z_side == 0 else p)
                    put(pl.ds(plane * padded_rows + spot, 1), both[line : line + 1])

    half_span = (knots_ref[0].astype(jnp.float32) - 1.0) * 0.5
    lane = lax.broadcasted_iota(jnp.int32, (ROWS, LANES), 1)
    tables = []
    scale = -math.log2(math.e) / (planes * slabs)
    for channel in range(4):
        if channel < 3:
            knot = [color_ref[channel, k] for k in range(KNOTS)]
        else:
            knot = [opacity_ref[k] * scale for k in range(KNOTS)]
        base = jnp.full((ROWS, LANES), knot[KNOTS - 1], jnp.float32)
        slope = jnp.zeros((ROWS, LANES), jnp.float32)
        for k in range(KNOTS - 1):
            rise = knot[k + 1] - knot[k]
            base = jnp.where(lane == k, knot[k] - k * rise, base)
            slope = jnp.where(lane == k, rise, slope)
        tables.append((base, slope))

    first_plane = slab * planes

    def pick(table, index):
        return jnp.take_along_axis(table, index, axis=1, mode="promise_in_bounds")

    row_blocks = rows // ROWS
    for copy in locals_[1:]:
        copy.wait()

    def send_part(turn):
        target = lax.rem(slab + 1 + turn, slabs)
        return pltpu.make_async_remote_copy(
            src_ref=part_ref.at[target], dst_ref=all_ref.at[slab], send_sem=part_send.at[target],
            recv_sem=part_recv.at[slab], device_id=(target, strip), device_id_type=MESH,
        )

    @pl.loop(0, slabs)
    def _(turn):
        target = lax.rem(slab + 1 + turn, slabs)

        @pl.loop(0, per_slab * row_blocks)
        def _(cell):
            inner = cell // row_blocks
            tile = target * per_slab + inner
            row = pl.multiple_of((cell % row_blocks) * ROWS, ROWS)
            column = pl.multiple_of(tile * LANES, LANES)
            near = near_ref[pl.ds(row, ROWS), pl.ds(column, LANES)] - first_plane
            far = far_ref[pl.ds(row, ROWS), pl.ds(column, LANES)] - first_plane

            def y_pass(plane):
                def at(ref, dy):
                    return ref[tile, pl.ds(row + (plane * padded_rows + PAD + dy), ROWS), :]

                mid, up, down = at(smooth_ref, 0), at(smooth_ref, 1), at(smooth_ref, -1)
                level = (up + down) + (mid + mid)
                step = up - down
                rise = (at(smooth_ref, 2) - at(smooth_ref, -2)) + (step + step)
                mid = at(slope_ref, 0)
                across = (at(slope_ref, 1) + at(slope_ref, -1)) + (mid + mid)
                return level, rise, across

            y = [y_pass(0)]
            pairs = []
            smooth = []
            seen = jnp.ones((ROWS, LANES), jnp.float32)
            image = [jnp.zeros((ROWS, LANES), jnp.float32) for _ in range(3)]
            for plane in range(1, total):
                y.append(y_pass(plane))
                pairs.append(tuple(a + b for a, b in zip(y[plane - 1], y[plane])))
                y[plane - 1] = None
                if plane < 2:
                    continue
                smooth.append(pairs[plane - 2][0] + pairs[plane - 1][0])
                if plane < 4:
                    continue
                z = plane - 4
                center = smooth[z + 1]
                grad_z = smooth[z + 2] - smooth[z]
                grad_y = pairs[z + 1][1] + pairs[z + 2][1]
                grad_x = pairs[z + 1][2] + pairs[z + 2][2]
                facing = 0.36 * grad_z + 0.45 * grad_y + 0.48 * grad_x
                magnitude = grad_z * grad_z + grad_y * grad_y + (grad_x * grad_x + 1.0)
                shading = 0.25 + jnp.abs(facing) * lax.rsqrt(magnitude)
                tf_level = jnp.tanh(0.75 * center) * half_span + half_span
                index = tf_level.astype(jnp.int32)
                color = [pick(base, index) + pick(slope, index) * tf_level for base, slope in tables]
                inside = (near <= z) & (far > z)
                through = jnp.exp2(jnp.where(inside, color[3], 0.0))
                after = seen * through
                weight = (seen - after) * shading
                seen = after
                image = [sum_ + c * weight for sum_, c in zip(image, color)]
            lanes = pl.ds(pl.multiple_of(inner * LANES, LANES), LANES)
            for channel, value in enumerate(image + [seen]):
                part_ref[target, channel, pl.ds(row, ROWS), lanes] = value

        @pl.when(turn < slabs - 1)
        def _():
            send_part(turn).start()

    all_ref[slab] = part_ref[slab]
    for number, (dz, dy) in enumerate(moves):
        @pl.when(exists(dz, dy))
        def _(dz=dz, dy=dy, number=number):
            rim(dz, dy, number, (slab + dz, strip + dy)).wait_send()
    for turn in range(slabs - 1):
        send_part(turn).wait_send()
    for turn in range(slabs - 1):
        source = lax.rem(slab + 1 + turn, slabs)
        pltpu.make_async_remote_copy(
            src_ref=part_ref.at[source], dst_ref=all_ref.at[source], send_sem=part_send.at[source],
            recv_sem=part_recv.at[source], device_id=(source, strip), device_id_type=MESH,
        ).wait_recv()
    color, seen = all_ref[slabs - 1, :3], all_ref[slabs - 1, 3]
    for other in range(slabs - 2, -1, -1):
        color = all_ref[other, :3] + all_ref[other, 3] * color
        seen = all_ref[other, 3] * seen
    out_ref[:3] = color
    out_ref[3] = 1.0 - seen


def on_device(volume_field, ray_near, ray_far, tf_color, tf_opacity, knot_count):
    planes, rows, columns = volume_field.shape
    slabs, strips = lax.axis_size("depth"), lax.axis_size("tile")
    edge = jnp.stack([volume_field[:, :2], volume_field[:, rows - 2 :]])
    edge = jnp.transpose(edge, (0, 2, 1, 3))
    tiles = columns // LANES
    smem = pl.BlockSpec(memory_space=pltpu.SMEM)
    anywhere = pl.BlockSpec(memory_space=pl.ANY)
    part = (slabs, 4, rows, columns // slabs)
    filtered = pltpu.VMEM((tiles, (planes + 4) * (rows + 2 * PAD), LANES), jnp.float32)
    return pl.pallas_call(
        functools.partial(render_kernel, (slabs, strips)),
        out_shape=jax.ShapeDtypeStruct(part[1:], jnp.float32),
        in_specs=[smem, smem, smem, anywhere, anywhere, anywhere, anywhere],
        out_specs=pl.BlockSpec(memory_space=pltpu.VMEM),
        scratch_shapes=[
            pltpu.VMEM(volume_field.shape, volume_field.dtype),
            pltpu.VMEM(ray_near.shape, ray_near.dtype),
            pltpu.VMEM(ray_far.shape, ray_far.dtype),
            pltpu.VMEM((2, 2, rows, columns), volume_field.dtype),
            pltpu.VMEM((2, 2, planes, columns), volume_field.dtype),
            pltpu.VMEM((2, 2, 2, 16, columns), volume_field.dtype),
            filtered,
            filtered,
            pltpu.VMEM(part, jnp.float32),
            pltpu.VMEM(part, jnp.float32),
            pltpu.SemaphoreType.DMA((3,)),
            pltpu.SemaphoreType.DMA((8,)),
            pltpu.SemaphoreType.DMA((8,)),
            pltpu.SemaphoreType.DMA((slabs,)),
            pltpu.SemaphoreType.DMA((slabs,)),
        ],
        compiler_params=pltpu.CompilerParams(
            collective_id=0, has_side_effects=True, vmem_limit_bytes=40 * 1024 * 1024
        ),
    )(tf_color, tf_opacity, knot_count, ray_near, ray_far, edge, volume_field)


def solution(mesh):
    return jax.shard_map(
        on_device,
        mesh=mesh,
        in_specs=(P("depth", "tile", None), P("tile", None), P("tile", None), P(), P(), P()),
        out_specs=P(None, "tile", "depth"),
        check_vma=False,
    )
```

```python
import functools
import math

import jax
import jax.numpy as jnp
from jax import lax
from jax.experimental import pallas as pl
from jax.experimental.pallas import tpu as pltpu
from jax.sharding import PartitionSpec as P

KNOTS = 16
LANES = 128
ROWS = 8
PAD = 8
MESH = pl.DeviceIdType.MESH


def x_window(tile, tiles):
    return max(tile - 1, 0), min(tile + 2, tiles)


def x_filters():
    shape = (3 * LANES, LANES)
    source = lax.broadcasted_iota(jnp.int32, shape, 0) - LANES
    offset = source - lax.broadcasted_iota(jnp.int32, shape, 1)
    distance = jnp.abs(offset)
    smooth = jnp.where(distance == 0, 0.125, jnp.where(distance == 1, 0.0625, 0.0))
    slope = jnp.where(distance == 1, 0.125, jnp.where(distance == 2, 0.0625, 0.0))
    slope = jnp.where(offset < 0, -slope, slope)
    return jnp.concatenate([smooth, slope], axis=1).astype(jnp.bfloat16)


def render_kernel(
    axes, color_ref, opacity_ref, knots_ref, near_hbm, far_hbm, edge_hbm, field_hbm, out_ref,
    field_ref, near_ref, far_ref, z_rim, y_rim, corner, smooth_ref, slope_ref, part_ref, all_ref,
    filter_ref, local_sem, rim_send, rim_recv, part_send, part_recv,
):
    slabs, strips = axes
    planes, rows, columns = field_ref.shape
    tiles = columns // LANES
    per_slab = tiles // slabs
    total = planes + 4
    padded_rows = rows + 2 * PAD
    slab, strip = lax.axis_index("depth"), lax.axis_index("tile")
    moves = [(dz, dy) for dz in (-1, 0, 1) for dy in (-1, 0, 1) if dz or dy]

    def exists(dz, dy):
        ok = None
        for step, mine, count in ((dz, slab, slabs), (dy, strip, strips)):
            if step:
                test = mine > 0 if step < 0 else mine < count - 1
                ok = test if ok is None else ok & test
        return ok

    locals_ = [
        pltpu.make_async_copy(source, target, local_sem.at[i])
        for i, (source, target) in enumerate(
            ((field_hbm, field_ref), (near_hbm, near_ref), (far_hbm, far_ref))
        )
    ]
    for copy in locals_:
        copy.start()

    barrier = pltpu.get_barrier_semaphore()
    arrivals = slabs - 1
    for step in range(1, slabs):
        pl.semaphore_signal(
            barrier, inc=1, device_id=(lax.rem(slab + step, slabs), strip), device_id_type=MESH
        )
    for dz, dy in moves:
        if dy:
            ok = exists(dz, dy)
            arrivals = arrivals + jnp.where(ok, 1, 0)

            @pl.when(ok)
            def _(dz=dz, dy=dy):
                pl.semaphore_signal(
                    barrier, inc=1, device_id=(slab + dz, strip + dy), device_id_type=MESH
                )
    filter_ref[...] = x_filters()
    pl.semaphore_wait(barrier, arrivals)

    def rim(dz, dy, number, target):
        z_side, y_side = (0 if dz > 0 else 1), (0 if dy > 0 else 1)
        if not dy:
            source = field_hbm.at[pl.ds(planes - 2 if dz > 0 else 0, 2)]
            place = z_rim.at[z_side]
        elif not dz:
            source, place = edge_hbm.at[1 - y_side], y_rim.at[y_side]
        else:
            source = edge_hbm.at[1 - y_side, :, pl.ds(planes - 16 if dz > 0 else 0, 16)]
            place = corner.at[z_side, y_side]
        return pltpu.make_async_remote_copy(
            src_ref=source, dst_ref=place, send_sem=rim_send.at[number],
            recv_sem=rim_recv.at[number], device_id=target, device_id_type=MESH,
        )

    for number, (dz, dy) in enumerate(moves):
        @pl.when(exists(dz, dy))
        def _(dz=dz, dy=dy, number=number):
            rim(dz, dy, number, (slab + dz, strip + dy)).start()

        @pl.when(jnp.logical_not(exists(-dz, -dy)))
        def _(dz=dz, dy=dy):
            z_side, y_side = (0 if dz > 0 else 1), (0 if dy > 0 else 1)
            if not dy:
                z_rim[z_side] = jnp.zeros(z_rim.shape[1:], z_rim.dtype)
            elif not dz:
                y_rim[y_side] = jnp.zeros(y_rim.shape[1:], y_rim.dtype)
            else:
                corner[z_side, y_side] = jnp.zeros(corner.shape[2:], corner.dtype)

    locals_[0].wait()
    group = 8
    for tile in range(tiles):
        first, last = x_window(tile, tiles)
        filters = filter_ref[(first - tile + 1) * LANES : (last - tile + 1) * LANES]

        @pl.loop(0, planes // group)
        def _(step, tile=tile, first=first, last=last, filters=filters):
            start = step * group
            window = field_ref[pl.ds(start, group), :, first * LANES : last * LANES]
            window = window.reshape(group * rows, (last - first) * LANES)
            both = jnp.dot(window, filters, preferred_element_type=jnp.float32)
            for i in range(group):
                at = pl.ds((start + (2 + i)) * padded_rows + PAD, rows)
                piece = both[i * rows : (i + 1) * rows]
                smooth_ref[tile, at, :] = piece[:, :LANES]
                slope_ref[tile, at, :] = piece[:, LANES:]

    for number, (dz, dy) in enumerate(moves):
        @pl.when(exists(-dz, -dy))
        def _(dz=dz, dy=dy, number=number):
            rim(dz, dy, number, (slab - dz, strip - dy)).wait_recv()

    for tile in range(tiles):
        first, last = x_window(tile, tiles)
        filters = filter_ref[(first - tile + 1) * LANES : (last - tile + 1) * LANES]
        lanes = slice(first * LANES, last * LANES)

        def filtered(window):
            window = window.reshape(-1, window.shape[-1])
            return jnp.dot(window, filters, preferred_element_type=jnp.float32)

        def put(at, piece, tile=tile):
            smooth_ref[tile, at, :] = piece[:, :LANES]
            slope_ref[tile, at, :] = piece[:, LANES:]

        both = filtered(z_rim[:, :, :, lanes])
        for i, plane in enumerate((0, 1, planes + 2, planes + 3)):
            put(pl.ds(plane * padded_rows + PAD, rows), both[i * rows : (i + 1) * rows])
        both = filtered(y_rim[:, :, :, lanes])
        spots = (PAD - 2, PAD - 1, PAD + rows, PAD + rows + 1)
        for i, spot in enumerate(spots):
            put(
                pl.ds(2 * padded_rows + spot, planes, stride=padded_rows),
                both[i * planes : (i + 1) * planes],
            )
        both = filtered(corner[:, :, :, :, lanes])
        for z_side in range(2):
            for i, spot in enumerate(spots):
                for p in range(2):
                    plane = p if z_side == 0 else planes + 2 + p
                    line = (z_side * 4 + i) * 16 + (14 + p if z_side == 0 else p)
                    put(pl.ds(plane * padded_rows + spot, 1), both[line : line + 1])

    half_span = (knots_ref[0].astype(jnp.float32) - 1.0) * 0.5
    lane = lax.broadcasted_iota(jnp.int32, (ROWS, LANES), 1)
    tables = []
    scale = -math.log2(math.e) / (planes * slabs)
    for channel in range(4):
        if channel < 3:
            knot = [color_ref[channel, k] for k in range(KNOTS)]
        else:
            knot = [opacity_ref[k] * scale for k in range(KNOTS)]
        base = jnp.full((ROWS, LANES), knot[KNOTS - 1], jnp.float32)
        slope = jnp.zeros((ROWS, LANES), jnp.float32)
        for k in range(KNOTS - 1):
            rise = knot[k + 1] - knot[k]
            base = jnp.where(lane == k, knot[k] - k * rise, base)
            slope = jnp.where(lane == k, rise, slope)
        tables.append((base, slope))

    first_plane = slab * planes

    def pick(table, index):
        return jnp.take_along_axis(table, index, axis=1, mode="promise_in_bounds")

    row_blocks = rows // ROWS
    for copy in locals_[1:]:
        copy.wait()

    def send_part(turn):
        target = lax.rem(slab + 1 + turn, slabs)
        return pltpu.make_async_remote_copy(
            src_ref=part_ref.at[target], dst_ref=all_ref.at[slab], send_sem=part_send.at[target],
            recv_sem=part_recv.at[slab], device_id=(target, strip), device_id_type=MESH,
        )

    @pl.loop(0, slabs)
    def _(turn):
        target = lax.rem(slab + 1 + turn, slabs)

        @pl.loop(0, per_slab * row_blocks)
        def _(cell):
            inner = cell // row_blocks
            tile = target * per_slab + inner
            row = pl.multiple_of((cell % row_blocks) * ROWS, ROWS)
            column = pl.multiple_of(tile * LANES, LANES)
            near = near_ref[pl.ds(row, ROWS), pl.ds(column, LANES)] - first_plane
            far = far_ref[pl.ds(row, ROWS), pl.ds(column, LANES)] - first_plane

            def y_pass(plane):
                def at(ref, dy):
                    return ref[tile, pl.ds(row + (plane * padded_rows + PAD + dy), ROWS), :]

                mid, up, down = at(smooth_ref, 0), at(smooth_ref, 1), at(smooth_ref, -1)
                level = (up + down) + (mid + mid)
                step = up - down
                rise = (at(smooth_ref, 2) - at(smooth_ref, -2)) + (step + step)
                mid = at(slope_ref, 0)
                across = (at(slope_ref, 1) + at(slope_ref, -1)) + (mid + mid)
                return level, rise, across

            y = [y_pass(0)]
            pairs = []
            smooth = []
            seen = jnp.ones((ROWS, LANES), jnp.float32)
            image = [jnp.zeros((ROWS, LANES), jnp.float32) for _ in range(3)]
            for plane in range(1, total):
                y.append(y_pass(plane))
                pairs.append(tuple(a + b for a, b in zip(y[plane - 1], y[plane])))
                y[plane - 1] = None
                if plane < 2:
                    continue
                smooth.append(pairs[plane - 2][0] + pairs[plane - 1][0])
                if plane < 4:
                    continue
                z = plane - 4
                center = smooth[z + 1]
                grad_z = smooth[z + 2] - smooth[z]
                grad_y = pairs[z + 1][1] + pairs[z + 2][1]
                grad_x = pairs[z + 1][2] + pairs[z + 2][2]
                facing = 0.36 * grad_z + 0.45 * grad_y + 0.48 * grad_x
                magnitude = grad_z * grad_z + grad_y * grad_y + (grad_x * grad_x + 1.0)
                shading = 0.25 + jnp.abs(facing) * lax.rsqrt(magnitude)
                tf_level = jnp.tanh(0.75 * center) * half_span + half_span
                index = tf_level.astype(jnp.int32)
                color = [pick(base, index) + pick(slope, index) * tf_level for base, slope in tables]
                inside = (near <= z) & (far > z)
                through = jnp.exp2(jnp.where(inside, color[3], 0.0))
                after = seen * through
                weight = (seen - after) * shading
                seen = after
                image = [sum_ + c * weight for sum_, c in zip(image, color)]
            lanes = pl.ds(pl.multiple_of(inner * LANES, LANES), LANES)
            for channel, value in enumerate(image + [seen]):
                part_ref[target, channel, pl.ds(row, ROWS), lanes] = value

        @pl.when(turn < slabs - 1)
        def _():
            send_part(turn).start()

    all_ref[slab] = part_ref[slab]
    for number, (dz, dy) in enumerate(moves):
        @pl.when(exists(dz, dy))
        def _(dz=dz, dy=dy, number=number):
            rim(dz, dy, number, (slab + dz, strip + dy)).wait_send()
    for turn in range(slabs - 1):
        send_part(turn).wait_send()
    for turn in range(slabs - 1):
        source = lax.rem(slab + 1 + turn, slabs)
        pltpu.make_async_remote_copy(
            src_ref=part_ref.at[source], dst_ref=all_ref.at[source], send_sem=part_send.at[source],
            recv_sem=part_recv.at[source], device_id=(source, strip), device_id_type=MESH,
        ).wait_recv()
    color, seen = all_ref[slabs - 1, :3], all_ref[slabs - 1, 3]
    for other in range(slabs - 2, -1, -1):
        color = all_ref[other, :3] + all_ref[other, 3] * color
        seen = all_ref[other, 3] * seen
    out_ref[:3] = color
    out_ref[3] = 1.0 - seen


def on_device(volume_field, ray_near, ray_far, tf_color, tf_opacity, knot_count):
    planes, rows, columns = volume_field.shape
    slabs, strips = lax.axis_size("depth"), lax.axis_size("tile")
    edge = jnp.stack([volume_field[:, :2], volume_field[:, rows - 2 :]])
    edge = jnp.transpose(edge, (0, 2, 1, 3))
    tiles = columns // LANES
    smem = pl.BlockSpec(memory_space=pltpu.SMEM)
    anywhere = pl.BlockSpec(memory_space=pl.ANY)
    part = (slabs, 4, rows, columns // slabs)
    filtered = pltpu.VMEM((tiles, (planes + 4) * (rows + 2 * PAD), LANES), jnp.float32)
    return pl.pallas_call(
        functools.partial(render_kernel, (slabs, strips)),
        out_shape=jax.ShapeDtypeStruct(part[1:], jnp.float32),
        in_specs=[smem, smem, smem, anywhere, anywhere, anywhere, anywhere],
        out_specs=pl.BlockSpec(memory_space=pltpu.VMEM),
        scratch_shapes=[
            pltpu.VMEM(volume_field.shape, volume_field.dtype),
            pltpu.VMEM(ray_near.shape, ray_near.dtype),
            pltpu.VMEM(ray_far.shape, ray_far.dtype),
            pltpu.VMEM((2, 2, rows, columns), volume_field.dtype),
            pltpu.VMEM((2, 2, planes, columns), volume_field.dtype),
            pltpu.VMEM((2, 2, 2, 16, columns), volume_field.dtype),
            filtered,
            filtered,
            pltpu.VMEM(part, jnp.float32),
            pltpu.VMEM(part, jnp.float32),
            pltpu.VMEM((3 * LANES, 2 * LANES), volume_field.dtype),
            pltpu.SemaphoreType.DMA((3,)),
            pltpu.SemaphoreType.DMA((8,)),
            pltpu.SemaphoreType.DMA((8,)),
            pltpu.SemaphoreType.DMA((slabs,)),
            pltpu.SemaphoreType.DMA((slabs,)),
        ],
        compiler_params=pltpu.CompilerParams(
            collective_id=0, has_side_effects=True, vmem_limit_bytes=60 * 1024 * 1024
        ),
    )(tf_color, tf_opacity, knot_count, ray_near, ray_far, edge, volume_field)


def solution(mesh):
    return jax.shard_map(
        on_device,
        mesh=mesh,
        in_specs=(P("depth", "tile", None), P("tile", None), P("tile", None), P(), P(), P()),
        out_specs=P(None, "tile", "depth"),
        check_vma=False,
    )
```

```python
import functools
import math

import jax
import jax.numpy as jnp
from jax import lax
from jax.experimental import pallas as pl
from jax.experimental.pallas import tpu as pltpu
from jax.sharding import PartitionSpec as P

KNOTS = 16
LANES = 128
ROWS = 8
PAD = 8
MESH = pl.DeviceIdType.MESH


def x_window(tile, tiles):
    return max(tile - 1, 0), min(tile + 2, tiles)


def x_filters():
    shape = (3 * LANES, LANES)
    source = lax.broadcasted_iota(jnp.int32, shape, 0) - LANES
    offset = source - lax.broadcasted_iota(jnp.int32, shape, 1)
    distance = jnp.abs(offset)
    smooth = jnp.where(distance == 0, 0.125, jnp.where(distance == 1, 0.0625, 0.0))
    slope = jnp.where(distance == 1, 0.125, jnp.where(distance == 2, 0.0625, 0.0))
    slope = jnp.where(offset < 0, -slope, slope)
    return jnp.concatenate([smooth, slope], axis=1).astype(jnp.bfloat16)


def render_kernel(
    axes, color_ref, opacity_ref, knots_ref, near_hbm, far_hbm, edge_hbm, field_hbm, out_ref,
    field_ref, near_ref, far_ref, z_rim, y_rim, corner, smooth_ref, slope_ref, part_ref, all_ref,
    filter_ref, local_sem, rim_send, rim_recv, part_send, part_recv,
):
    slabs, strips = axes
    planes, rows, columns = field_ref.shape
    tiles = columns // LANES
    per_slab = tiles // slabs
    total = planes + 4
    padded_rows = rows + 2 * PAD
    slab, strip = lax.axis_index("depth"), lax.axis_index("tile")
    moves = [(dz, dy) for dz in (-1, 0, 1) for dy in (-1, 0, 1) if dz or dy]

    def exists(dz, dy):
        ok = None
        for step, mine, count in ((dz, slab, slabs), (dy, strip, strips)):
            if step:
                test = mine > 0 if step < 0 else mine < count - 1
                ok = test if ok is None else ok & test
        return ok

    locals_ = [
        pltpu.make_async_copy(source, target, local_sem.at[i])
        for i, (source, target) in enumerate(
            ((field_hbm, field_ref), (near_hbm, near_ref), (far_hbm, far_ref))
        )
    ]
    for copy in locals_:
        copy.start()

    barrier = pltpu.get_barrier_semaphore()
    arrivals = slabs - 1
    for step in range(1, slabs):
        pl.semaphore_signal(
            barrier, inc=1, device_id=(lax.rem(slab + step, slabs), strip), device_id_type=MESH
        )
    for dz, dy in moves:
        if dy:
            ok = exists(dz, dy)
            arrivals = arrivals + jnp.where(ok, 1, 0)

            @pl.when(ok)
            def _(dz=dz, dy=dy):
                pl.semaphore_signal(
                    barrier, inc=1, device_id=(slab + dz, strip + dy), device_id_type=MESH
                )
    filter_ref[...] = x_filters()

    def rim(dz, dy, number, target):
        z_side, y_side = (0 if dz > 0 else 1), (0 if dy > 0 else 1)
        if not dy:
            source = field_hbm.at[pl.ds(planes - 2 if dz > 0 else 0, 2)]
            place = z_rim.at[z_side]
        elif not dz:
            source, place = edge_hbm.at[1 - y_side], y_rim.at[y_side]
        else:
            source = edge_hbm.at[1 - y_side, :, pl.ds(planes - 16 if dz > 0 else 0, 16)]
            place = corner.at[z_side, y_side]
        return pltpu.make_async_remote_copy(
            src_ref=source, dst_ref=place, send_sem=rim_send.at[number],
            recv_sem=rim_recv.at[number], device_id=target, device_id_type=MESH,
        )

    locals_[0].wait()
    group = 8
    for tile in range(tiles):
        if tile == tiles // 8:
            pl.semaphore_wait(barrier, arrivals)

            for number, (dz, dy) in enumerate(moves):
                @pl.when(exists(dz, dy))
                def _(dz=dz, dy=dy, number=number):
                    rim(dz, dy, number, (slab + dz, strip + dy)).start()

                @pl.when(jnp.logical_not(exists(-dz, -dy)))
                def _(dz=dz, dy=dy):
                    z_side, y_side = (0 if dz > 0 else 1), (0 if dy > 0 else 1)
                    if not dy:
                        z_rim[z_side] = jnp.zeros(z_rim.shape[1:], z_rim.dtype)
                    elif not dz:
                        y_rim[y_side] = jnp.zeros(y_rim.shape[1:], y_rim.dtype)
                    else:
                        corner[z_side, y_side] = jnp.zeros(corner.shape[2:], corner.dtype)

        first, last = x_window(tile, tiles)
        filters = filter_ref[(first - tile + 1) * LANES : (last - tile + 1) * LANES]

        @pl.loop(0, planes // group)
        def _(step, tile=tile, first=first, last=last, filters=filters):
            start = step * group
            window = field_ref[pl.ds(start, group), :, first * LANES : last * LANES]
            window = window.reshape(group * rows, (last - first) * LANES)
            both = jnp.dot(window, filters, preferred_element_type=jnp.float32)
            for i in range(group):
                at = pl.ds((start + (2 + i)) * padded_rows + PAD, rows)
                piece = both[i * rows : (i + 1) * rows]
                smooth_ref[tile, at, :] = piece[:, :LANES]
                slope_ref[tile, at, :] = piece[:, LANES:]

    for number, (dz, dy) in enumerate(moves):
        @pl.when(exists(-dz, -dy))
        def _(dz=dz, dy=dy, number=number):
            rim(dz, dy, number, (slab - dz, strip - dy)).wait_recv()

    for tile in range(tiles):
        first, last = x_window(tile, tiles)
        filters = filter_ref[(first - tile + 1) * LANES : (last - tile + 1) * LANES]
        lanes = slice(first * LANES, last * LANES)

        def filtered(window):
            window = window.reshape(-1, window.shape[-1])
            return jnp.dot(window, filters, preferred_element_type=jnp.float32)

        def put(at, piece, tile=tile):
            smooth_ref[tile, at, :] = piece[:, :LANES]
            slope_ref[tile, at, :] = piece[:, LANES:]

        both = filtered(z_rim[:, :, :, lanes])
        for i, plane in enumerate((0, 1, planes + 2, planes + 3)):
            put(pl.ds(plane * padded_rows + PAD, rows), both[i * rows : (i + 1) * rows])
        both = filtered(y_rim[:, :, :, lanes])
        spots = (PAD - 2, PAD - 1, PAD + rows, PAD + rows + 1)
        for i, spot in enumerate(spots):
            put(
                pl.ds(2 * padded_rows + spot, planes, stride=padded_rows),
                both[i * planes : (i + 1) * planes],
            )
        both = filtered(corner[:, :, :, :, lanes])
        for z_side in range(2):
            for i, spot in enumerate(spots):
                for p in range(2):
                    plane = p if z_side == 0 else planes + 2 + p
                    line = (z_side * 4 + i) * 16 + (14 + p if z_side == 0 else p)
                    put(pl.ds(plane * padded_rows + spot, 1), both[line : line + 1])

    half_span = (knots_ref[0].astype(jnp.float32) - 1.0) * 0.5
    lane = lax.broadcasted_iota(jnp.int32, (ROWS, LANES), 1)
    tables = []
    scale = -math.log2(math.e) / (planes * slabs)
    for channel in range(4):
        if channel < 3:
            knot = [color_ref[channel, k] for k in range(KNOTS)]
        else:
            knot = [opacity_ref[k] * scale for k in range(KNOTS)]
        base = jnp.full((ROWS, LANES), knot[KNOTS - 1], jnp.float32)
        slope = jnp.zeros((ROWS, LANES), jnp.float32)
        for k in range(KNOTS - 1):
            rise = knot[k + 1] - knot[k]
            base = jnp.where(lane == k, knot[k] - k * rise, base)
            slope = jnp.where(lane == k, rise, slope)
        tables.append((base, slope))

    first_plane = slab * planes

    def pick(table, index):
        return jnp.take_along_axis(table, index, axis=1, mode="promise_in_bounds")

    row_blocks = rows // ROWS
    for copy in locals_[1:]:
        copy.wait()

    def send_part(target, source, inner):
        return pltpu.make_async_remote_copy(
            src_ref=part_ref.at[target, inner], dst_ref=all_ref.at[source, inner],
            send_sem=part_send.at[target, inner], recv_sem=part_recv.at[source, inner],
            device_id=(target, strip), device_id_type=MESH,
        )

    @pl.loop(0, slabs * per_slab)
    def _(turn):
        target = lax.rem(slab + 1 + turn // per_slab, slabs)
        inner = turn % per_slab

        @pl.loop(0, row_blocks)
        def _(cell):
            tile = target * per_slab + inner
            row = pl.multiple_of(cell * ROWS, ROWS)
            column = pl.multiple_of(tile * LANES, LANES)
            near = near_ref[pl.ds(row, ROWS), pl.ds(column, LANES)] - first_plane
            far = far_ref[pl.ds(row, ROWS), pl.ds(column, LANES)] - first_plane

            def y_pass(plane):
                def at(ref, dy):
                    return ref[tile, pl.ds(row + (plane * padded_rows + PAD + dy), ROWS), :]

                mid, up, down = at(smooth_ref, 0), at(smooth_ref, 1), at(smooth_ref, -1)
                level = (up + down) + (mid + mid)
                step = up - down
                rise = (at(smooth_ref, 2) - at(smooth_ref, -2)) + (step + step)
                mid = at(slope_ref, 0)
                across = (at(slope_ref, 1) + at(slope_ref, -1)) + (mid + mid)
                return level, rise, across

            y = [y_pass(0)]
            pairs = []
            smooth = []
            seen = jnp.ones((ROWS, LANES), jnp.float32)
            image = [jnp.zeros((ROWS, LANES), jnp.float32) for _ in range(3)]
            for plane in range(1, total):
                y.append(y_pass(plane))
                pairs.append(tuple(a + b for a, b in zip(y[plane - 1], y[plane])))
                y[plane - 1] = None
                if plane < 2:
                    continue
                smooth.append(pairs[plane - 2][0] + pairs[plane - 1][0])
                if plane < 4:
                    continue
                z = plane - 4
                center = smooth[z + 1]
                grad_z = smooth[z + 2] - smooth[z]
                grad_y = pairs[z + 1][1] + pairs[z + 2][1]
                grad_x = pairs[z + 1][2] + pairs[z + 2][2]
                facing = 0.36 * grad_z + 0.45 * grad_y + 0.48 * grad_x
                magnitude = grad_z * grad_z + grad_y * grad_y + (grad_x * grad_x + 1.0)
                shading = 0.25 + jnp.abs(facing) * lax.rsqrt(magnitude)
                tf_level = jnp.tanh(0.75 * center) * half_span + half_span
                index = tf_level.astype(jnp.int32)
                color = [pick(base, index) + pick(slope, index) * tf_level for base, slope in tables]
                inside = (near <= z) & (far > z)
                through = jnp.exp2(jnp.where(inside, color[3], 0.0))
                after = seen * through
                weight = (seen - after) * shading
                seen = after
                image = [sum_ + c * weight for sum_, c in zip(image, color)]
            for channel, value in enumerate(image + [seen]):
                part_ref[target, inner, channel, pl.ds(row, ROWS), :] = value

        @pl.when(turn < (slabs - 1) * per_slab)
        def _():
            send_part(target, slab, inner).start()

    all_ref[slab] = part_ref[slab]
    for number, (dz, dy) in enumerate(moves):
        @pl.when(exists(dz, dy))
        def _(dz=dz, dy=dy, number=number):
            rim(dz, dy, number, (slab + dz, strip + dy)).wait_send()
    others = [lax.rem(slab + 1 + turn, slabs) for turn in range(slabs - 1)]
    for inner in range(per_slab):
        for other in others:
            send_part(other, slab, inner).wait_send()
        for other in others:
            send_part(other, other, inner).wait_recv()
    for inner in range(per_slab):
        lanes = slice(inner * LANES, (inner + 1) * LANES)
        color, seen = all_ref[slabs - 1, inner, :3], all_ref[slabs - 1, inner, 3]
        for other in range(slabs - 2, -1, -1):
            color = all_ref[other, inner, :3] + all_ref[other, inner, 3] * color
            seen = all_ref[other, inner, 3] * seen
        out_ref[:3, :, lanes] = color
        out_ref[3, :, lanes] = 1.0 - seen


def on_device(volume_field, ray_near, ray_far, tf_color, tf_opacity, knot_count):
    planes, rows, columns = volume_field.shape
    slabs, strips = lax.axis_size("depth"), lax.axis_size("tile")
    edge = jnp.stack([volume_field[:, :2], volume_field[:, rows - 2 :]])
    edge = jnp.transpose(edge, (0, 2, 1, 3))
    tiles = columns // LANES
    smem = pl.BlockSpec(memory_space=pltpu.SMEM)
    anywhere = pl.BlockSpec(memory_space=pl.ANY)
    per_slab = tiles // slabs
    part = (slabs, per_slab, 4, rows, LANES)
    filtered = pltpu.VMEM((tiles, (planes + 4) * (rows + 2 * PAD), LANES), jnp.float32)
    return pl.pallas_call(
        functools.partial(render_kernel, (slabs, strips)),
        out_shape=jax.ShapeDtypeStruct((4, rows, columns // slabs), jnp.float32),
        in_specs=[smem, smem, smem, anywhere, anywhere, anywhere, anywhere],
        out_specs=pl.BlockSpec(memory_space=pltpu.VMEM),
        scratch_shapes=[
            pltpu.VMEM(volume_field.shape, volume_field.dtype),
            pltpu.VMEM(ray_near.shape, ray_near.dtype),
            pltpu.VMEM(ray_far.shape, ray_far.dtype),
            pltpu.VMEM((2, 2, rows, columns), volume_field.dtype),
            pltpu.VMEM((2, 2, planes, columns), volume_field.dtype),
            pltpu.VMEM((2, 2, 2, 16, columns), volume_field.dtype),
            filtered,
            filtered,
            pltpu.VMEM(part, jnp.float32),
            pltpu.VMEM(part, jnp.float32),
            pltpu.VMEM((3 * LANES, 2 * LANES), volume_field.dtype),
            pltpu.SemaphoreType.DMA((3,)),
            pltpu.SemaphoreType.DMA((8,)),
            pltpu.SemaphoreType.DMA((8,)),
            pltpu.SemaphoreType.DMA((slabs, per_slab)),
            pltpu.SemaphoreType.DMA((slabs, per_slab)),
        ],
        compiler_params=pltpu.CompilerParams(
            collective_id=0, has_side_effects=True, vmem_limit_bytes=60 * 1024 * 1024
        ),
    )(tf_color, tf_opacity, knot_count, ray_near, ray_far, edge, volume_field)


def solution(mesh):
    return jax.shard_map(
        on_device,
        mesh=mesh,
        in_specs=(P("depth", "tile", None), P("tile", None), P("tile", None), P(), P(), P()),
        out_specs=P(None, "tile", "depth"),
        check_vma=False,
    )
```

```python
import functools
import math

import jax
import jax.numpy as jnp
from jax import lax
from jax.experimental import pallas as pl
from jax.experimental.pallas import tpu as pltpu
from jax.sharding import PartitionSpec as P

KNOTS = 16
LANES = 128
ROWS = 8
PAD = 8
MESH = pl.DeviceIdType.MESH


def x_window(tile, tiles):
    return max(tile - 1, 0), min(tile + 2, tiles)


def x_filters():
    shape = (3 * LANES, LANES)
    source = lax.broadcasted_iota(jnp.int32, shape, 0) - LANES
    offset = source - lax.broadcasted_iota(jnp.int32, shape, 1)
    distance = jnp.abs(offset)
    smooth = jnp.where(distance == 0, 0.125, jnp.where(distance == 1, 0.0625, 0.0))
    slope = jnp.where(distance == 1, 0.125, jnp.where(distance == 2, 0.0625, 0.0))
    slope = jnp.where(offset < 0, -slope, slope)
    return jnp.concatenate([smooth, slope], axis=1).astype(jnp.bfloat16)


def render_kernel(
    axes, color_ref, opacity_ref, knots_ref, near_hbm, far_hbm, edge_hbm, field_hbm, out_ref,
    field_ref, near_ref, far_ref, z_rim, y_rim, corner, smooth_ref, slope_ref, part_ref, all_ref, stage_ref,
    filter_ref, local_sem, rim_send, rim_recv, part_send, part_recv,
):
    slabs, strips = axes
    planes, rows, columns = field_ref.shape
    tiles = columns // LANES
    per_slab = tiles // slabs
    total = planes + 4
    padded_rows = rows + 2 * PAD
    slab, strip = lax.axis_index("depth"), lax.axis_index("tile")
    moves = [(dz, dy) for dz in (-1, 0, 1) for dy in (-1, 0, 1) if dz or dy]

    def exists(dz, dy):
        ok = None
        for step, mine, count in ((dz, slab, slabs), (dy, strip, strips)):
            if step:
                test = mine > 0 if step < 0 else mine < count - 1
                ok = test if ok is None else ok & test
        return ok

    locals_ = [
        pltpu.make_async_copy(source, target, local_sem.at[i])
        for i, (source, target) in enumerate(
            ((field_hbm, field_ref), (near_hbm, near_ref), (far_hbm, far_ref))
        )
    ]
    for copy in locals_:
        copy.start()

    barrier = pltpu.get_barrier_semaphore()
    arrivals = slabs - 1
    for step in range(1, slabs):
        pl.semaphore_signal(
            barrier, inc=1, device_id=(lax.rem(slab + step, slabs), strip), device_id_type=MESH
        )
    for dz, dy in moves:
        if dy:
            ok = exists(dz, dy)
            arrivals = arrivals + jnp.where(ok, 1, 0)

            @pl.when(ok)
            def _(dz=dz, dy=dy):
                pl.semaphore_signal(
                    barrier, inc=1, device_id=(slab + dz, strip + dy), device_id_type=MESH
                )
    filter_ref[...] = x_filters()

    def rim(dz, dy, number, target):
        z_side, y_side = (0 if dz > 0 else 1), (0 if dy > 0 else 1)
        if not dy:
            source = field_hbm.at[pl.ds(planes - 2 if dz > 0 else 0, 2)]
            place = z_rim.at[z_side]
        elif not dz:
            source, place = edge_hbm.at[1 - y_side], y_rim.at[y_side]
        else:
            source = edge_hbm.at[1 - y_side, :, pl.ds(planes - 16 if dz > 0 else 0, 16)]
            place = corner.at[z_side, y_side]
        return pltpu.make_async_remote_copy(
            src_ref=source, dst_ref=place, send_sem=rim_send.at[number],
            recv_sem=rim_recv.at[number], device_id=target, device_id_type=MESH,
        )

    locals_[0].wait()
    group = 8
    for tile in range(tiles):
        if tile == tiles // 8:
            pl.semaphore_wait(barrier, arrivals)

            for number, (dz, dy) in enumerate(moves):
                @pl.when(exists(dz, dy))
                def _(dz=dz, dy=dy, number=number):
                    rim(dz, dy, number, (slab + dz, strip + dy)).start()

                @pl.when(jnp.logical_not(exists(-dz, -dy)))
                def _(dz=dz, dy=dy):
                    z_side, y_side = (0 if dz > 0 else 1), (0 if dy > 0 else 1)
                    if not dy:
                        z_rim[z_side] = jnp.zeros(z_rim.shape[1:], z_rim.dtype)
                    elif not dz:
                        y_rim[y_side] = jnp.zeros(y_rim.shape[1:], y_rim.dtype)
                    else:
                        corner[z_side, y_side] = jnp.zeros(corner.shape[2:], corner.dtype)

        first, last = x_window(tile, tiles)
        filters = filter_ref[(first - tile + 1) * LANES : (last - tile + 1) * LANES]

        @pl.loop(0, planes // group)
        def _(step, tile=tile, first=first, last=last, filters=filters):
            start = step * group
            window = field_ref[pl.ds(start, group), :, first * LANES : last * LANES]
            window = window.reshape(group * rows, (last - first) * LANES)
            both = jnp.dot(window, filters, preferred_element_type=jnp.float32)
            for i in range(group):
                at = pl.ds((start + (2 + i)) * padded_rows + PAD, rows)
                piece = both[i * rows : (i + 1) * rows]
                smooth_ref[tile, at, :] = piece[:, :LANES]
                slope_ref[tile, at, :] = piece[:, LANES:]

    for number, (dz, dy) in enumerate(moves):
        @pl.when(exists(-dz, -dy))
        def _(dz=dz, dy=dy, number=number):
            rim(dz, dy, number, (slab - dz, strip - dy)).wait_recv()

    for tile in range(tiles):
        first, last = x_window(tile, tiles)
        filters = filter_ref[(first - tile + 1) * LANES : (last - tile + 1) * LANES]
        lanes = slice(first * LANES, last * LANES)

        def filtered(window):
            window = window.reshape(-1, window.shape[-1])
            return jnp.dot(window, filters, preferred_element_type=jnp.float32)

        def put(at, piece, tile=tile):
            smooth_ref[tile, at, :] = piece[:, :LANES]
            slope_ref[tile, at, :] = piece[:, LANES:]

        both = filtered(z_rim[:, :, :, lanes])
        for i, plane in enumerate((0, 1, planes + 2, planes + 3)):
            put(pl.ds(plane * padded_rows + PAD, rows), both[i * rows : (i + 1) * rows])
        both = filtered(y_rim[:, :, :, lanes])
        spots = (PAD - 2, PAD - 1, PAD + rows, PAD + rows + 1)
        for i, spot in enumerate(spots):
            put(
                pl.ds(2 * padded_rows + spot, planes, stride=padded_rows),
                both[i * planes : (i + 1) * planes],
            )
        both = filtered(corner[:, :, :, :, lanes])
        for z_side in range(2):
            for i, spot in enumerate(spots):
                for p in range(2):
                    plane = p if z_side == 0 else planes + 2 + p
                    line = (z_side * 4 + i) * 16 + (14 + p if z_side == 0 else p)
                    put(pl.ds(plane * padded_rows + spot, 1), both[line : line + 1])

    half_span = (knots_ref[0].astype(jnp.float32) - 1.0) * 0.5
    lane = lax.broadcasted_iota(jnp.int32, (ROWS, LANES), 1)
    tables = []
    scale = -math.log2(math.e) / (planes * slabs)
    for channel in range(4):
        if channel < 3:
            knot = [color_ref[channel, k] for k in range(KNOTS)]
        else:
            knot = [opacity_ref[k] * scale for k in range(KNOTS)]
        base = jnp.full((ROWS, LANES), knot[KNOTS - 1], jnp.float32)
        slope = jnp.zeros((ROWS, LANES), jnp.float32)
        for k in range(KNOTS - 1):
            rise = knot[k + 1] - knot[k]
            base = jnp.where(lane == k, knot[k] - k * rise, base)
            slope = jnp.where(lane == k, rise, slope)
        tables.append((base, slope))

    first_plane = slab * planes

    def pick(table, index):
        return jnp.take_along_axis(table, index, axis=1, mode="promise_in_bounds")

    row_blocks = rows // ROWS
    for copy in locals_[1:]:
        copy.wait()

    def send_part(target, source, inner):
        return pltpu.make_async_remote_copy(
            src_ref=part_ref.at[target, inner], dst_ref=all_ref.at[source, inner],
            send_sem=part_send.at[target, inner], recv_sem=part_recv.at[source, inner],
            device_id=(target, strip), device_id_type=MESH,
        )

    @pl.loop(0, slabs * per_slab)
    def _(turn):
        target = lax.rem(slab + 1 + turn // per_slab, slabs)
        inner = turn % per_slab

        @pl.loop(0, row_blocks)
        def _(cell):
            tile = target * per_slab + inner
            row = pl.multiple_of(cell * ROWS, ROWS)
            column = pl.multiple_of(tile * LANES, LANES)
            near = near_ref[pl.ds(row, ROWS), pl.ds(column, LANES)] - first_plane
            far = far_ref[pl.ds(row, ROWS), pl.ds(column, LANES)] - first_plane

            def y_pass(plane):
                def at(ref, dy):
                    return ref[tile, pl.ds(row + (plane * padded_rows + PAD + dy), ROWS), :]

                mid, up, down = at(smooth_ref, 0), at(smooth_ref, 1), at(smooth_ref, -1)
                level = (up + down) + (mid + mid)
                step = up - down
                rise = (at(smooth_ref, 2) - at(smooth_ref, -2)) + (step + step)
                mid = at(slope_ref, 0)
                across = (at(slope_ref, 1) + at(slope_ref, -1)) + (mid + mid)
                return level, rise, across

            y = [y_pass(0)]
            pairs = []
            smooth = []
            seen = jnp.ones((ROWS, LANES), jnp.float32)
            image = [jnp.zeros((ROWS, LANES), jnp.float32) for _ in range(3)]
            for plane in range(1, total):
                y.append(y_pass(plane))
                pairs.append(tuple(a + b for a, b in zip(y[plane - 1], y[plane])))
                y[plane - 1] = None
                if plane < 2:
                    continue
                smooth.append(pairs[plane - 2][0] + pairs[plane - 1][0])
                if plane < 4:
                    continue
                z = plane - 4
                center = smooth[z + 1]
                grad_z = smooth[z + 2] - smooth[z]
                grad_y = pairs[z + 1][1] + pairs[z + 2][1]
                grad_x = pairs[z + 1][2] + pairs[z + 2][2]
                facing = 0.36 * grad_z + 0.45 * grad_y + 0.48 * grad_x
                magnitude = grad_z * grad_z + grad_y * grad_y + (grad_x * grad_x + 1.0)
                shading = 0.25 + jnp.abs(facing) * lax.rsqrt(magnitude)
                tf_level = jnp.tanh(0.75 * center) * half_span + half_span
                index = tf_level.astype(jnp.int32)
                color = [pick(base, index) + pick(slope, index) * tf_level for base, slope in tables]
                inside = (near <= z) & (far > z)
                through = jnp.exp2(jnp.where(inside, color[3], 0.0))
                after = seen * through
                weight = (seen - after) * shading
                seen = after
                image = [sum_ + c * weight for sum_, c in zip(image, color)]
            for channel, value in enumerate(image + [seen]):
                stage_ref[channel, pl.ds(row, ROWS), :] = value

        level = jnp.minimum(stage_ref[...], 1.0) * 65534.0 - 32766.5
        part_ref[target, inner] = jnp.floor(level).astype(jnp.int32).astype(jnp.int16)

        @pl.when(turn < (slabs - 1) * per_slab)
        def _():
            send_part(target, slab, inner).start()

    all_ref[slab] = part_ref[slab]
    for number, (dz, dy) in enumerate(moves):
        @pl.when(exists(dz, dy))
        def _(dz=dz, dy=dy, number=number):
            rim(dz, dy, number, (slab + dz, strip + dy)).wait_send()
    others = [lax.rem(slab + 1 + turn, slabs) for turn in range(slabs - 1)]
    for inner in range(per_slab):
        for other in others:
            send_part(other, slab, inner).wait_send()
        for other in others:
            send_part(other, other, inner).wait_recv()
    for inner in range(per_slab):
        lanes = slice(inner * LANES, (inner + 1) * LANES)
        level = all_ref[:, inner].astype(jnp.int32).astype(jnp.float32)
        level = (level + 32767.0) * (1.0 / 65534.0)
        color, seen = level[slabs - 1, :3], level[slabs - 1, 3]
        for other in range(slabs - 2, -1, -1):
            color = level[other, :3] + level[other, 3] * color
            seen = level[other, 3] * seen
        out_ref[:3, :, lanes] = color
        out_ref[3, :, lanes] = 1.0 - seen


def on_device(volume_field, ray_near, ray_far, tf_color, tf_opacity, knot_count):
    planes, rows, columns = volume_field.shape
    slabs, strips = lax.axis_size("depth"), lax.axis_size("tile")
    edge = jnp.stack([volume_field[:, :2], volume_field[:, rows - 2 :]])
    edge = jnp.transpose(edge, (0, 2, 1, 3))
    tiles = columns // LANES
    smem = pl.BlockSpec(memory_space=pltpu.SMEM)
    anywhere = pl.BlockSpec(memory_space=pl.ANY)
    per_slab = tiles // slabs
    part = (slabs, per_slab, 4, rows, LANES)
    filtered = pltpu.VMEM((tiles, (planes + 4) * (rows + 2 * PAD), LANES), jnp.float32)
    return pl.pallas_call(
        functools.partial(render_kernel, (slabs, strips)),
        out_shape=jax.ShapeDtypeStruct((4, rows, columns // slabs), jnp.float32),
        in_specs=[smem, smem, smem, anywhere, anywhere, anywhere, anywhere],
        out_specs=pl.BlockSpec(memory_space=pltpu.VMEM),
        scratch_shapes=[
            pltpu.VMEM(volume_field.shape, volume_field.dtype),
            pltpu.VMEM(ray_near.shape, ray_near.dtype),
            pltpu.VMEM(ray_far.shape, ray_far.dtype),
            pltpu.VMEM((2, 2, rows, columns), volume_field.dtype),
            pltpu.VMEM((2, 2, planes, columns), volume_field.dtype),
            pltpu.VMEM((2, 2, 2, 16, columns), volume_field.dtype),
            filtered,
            filtered,
            pltpu.VMEM(part, jnp.int16),
            pltpu.VMEM(part, jnp.int16),
            pltpu.VMEM(part[2:], jnp.float32),
            pltpu.VMEM((3 * LANES, 2 * LANES), volume_field.dtype),
            pltpu.SemaphoreType.DMA((3,)),
            pltpu.SemaphoreType.DMA((8,)),
            pltpu.SemaphoreType.DMA((8,)),
            pltpu.SemaphoreType.DMA((slabs, per_slab)),
            pltpu.SemaphoreType.DMA((slabs, per_slab)),
        ],
        compiler_params=pltpu.CompilerParams(
            collective_id=0, has_side_effects=True, vmem_limit_bytes=60 * 1024 * 1024
        ),
    )(tf_color, tf_opacity, knot_count, ray_near, ray_far, edge, volume_field)


def solution(mesh):
    return jax.shard_map(
        on_device,
        mesh=mesh,
        in_specs=(P("depth", "tile", None), P("tile", None), P("tile", None), P(), P(), P()),
        out_specs=P(None, "tile", "depth"),
        check_vma=False,
    )
```
